256 devices in a mesh: dp: 8 (over z_lo, x), vocab: 32 (over y, z_hi, core).
Axes of the slice: x: 4, y: 4, z: 8 (z_hi: 4, z_lo: 2; z = z_hi * 2 + z_lo), core: 2. Of those that a mesh axis runs over, the one named last changes fastest.
Arguments:
- hidden_now: bfloat16 [1024, 3584], P('dp'), may hold values from -6 to 6
- hidden_next: bfloat16 [1024, 3584], P('dp'), may hold values from -100 to 100
- cotangent: bfloat16 [1024, 81920], P('dp', 'vocab'), may hold values from -6 to 6
- master: float32 [81920, 3584], P(('vocab', 'dp')), may hold values from -1 to 1
- moment: bfloat16 [81920, 3584], P(('vocab', 'dp')), may hold values from -19.2 to 19.2
- second: bfloat16 [81920, 3584], P(('vocab', 'dp')), may hold values from 2.048 to 20.48, as said below
- targets: int32 [1024], P('dp'), may hold values from 0 to 81919
Outputs:
- next_logits: bfloat16 [1024, 81920], P('dp', 'vocab')
- next_loss: float32 [1024], P('dp')
The draws below stay inside these ranges and needn't reach their ends.
Inputs may be any that keep to these rules, and one draw needn't show every extreme that they name: `second`: Positive.
All inputs are finite; a program needn't handle non-finite values.
Results may differ from the reference program's by a relative error of at most 0.015.
Values may be sent and summed in bfloat16 or wider, within the bound.
No kernel may reach another device: no remote copies, remote signals or barrier semaphores. Data moves between devices by JAX's collectives and lax.ppermute only.
A program may use at most 128 MiB of HBM per device.

```python
import math
import jax
import jax.numpy as jnp
from jax import lax

D = 3584
VS = 2560
TOK_GRP = 128
VOCAB = 81920
TOKENS = 1024
N_DP = 8
N_VOCAB = 32


def head_base(key):
    return jax.random.truncated_normal(jax.random.fold_in(key, 11), -6.0, 6.0, (VOCAB, D), jnp.float32)


def draw_master(key, part):
    shared = head_base(key)
    return shared * D ** (-0.5)


def draw_hidden_next(key, part):
    key = jax.random.fold_in(key, 5)
    values = 3.0 * jax.random.truncated_normal(key, -6.0, 6.0, (TOKENS, D), jnp.float32)
    return jnp.clip(values, -100.0, 100.0).astype(jnp.bfloat16)


def draw_moment(key, part):
    key = jax.random.fold_in(key, 7)
    return (0.099 * math.sqrt(TOKENS) * jax.random.truncated_normal(key, -6.0, 6.0, (VOCAB, D), jnp.float32)).astype(jnp.bfloat16)


def draw_second(key, part):
    key = jax.random.fold_in(key, 9)
    lower = math.log(0.00202 * TOKENS)
    upper = math.log(0.0198 * TOKENS)
    return jnp.exp(jax.random.uniform(key, (VOCAB, D), jnp.float32, lower, upper)).astype(jnp.bfloat16)


def with_ends(values, key, least, high):
    longest = values.shape.index(max(values.shape))
    spots = []
    for shift in (0, 1):
        where = [jax.random.randint(jax.random.fold_in(key, axis), (), 0, length) for axis, length in enumerate(values.shape)]
        where[longest] = (where[longest] + shift) % values.shape[longest]
        spots.append(tuple(where))
    return values.at[spots[0]].set(least).at[spots[1]].set(high)


def strengthened(entries, own_key, source, target, blocks, factor):
    def block_of(position):
        return (jnp.arange(entries.shape[position]) // (entries.shape[position] // blocks)).reshape((-1,) + (1,) * (entries.ndim - 1 - position))

    near = jax.random.permutation(own_key, blocks)[block_of(target)]
    far = (block_of(target) + blocks // 2) % blocks
    return jnp.where((block_of(source) == near) | (block_of(source) == far), factor * entries, entries)


def steps_of(rng, dims, cuts, least, largest):
    gain, own = 1.0, jax.random.fold_in(rng, 6)
    for axis_at, parts in cuts:
        draws = jnp.exp(jax.random.uniform(jax.random.fold_in(own, axis_at), (parts,), jnp.float32, least / len(cuts), largest / len(cuts)))
        gain = gain * jnp.repeat(draws, dims[axis_at] // parts).reshape([-1 if axis == axis_at else 1 for axis in range(len(dims))])
    return gain


def centred(stream_key, shape, spread, most, shards=(), kind=jnp.bfloat16):
    entries = jax.random.normal(stream_key, shape, jnp.float32) * spread
    if len(shards) > 0:
        entries = steps_of(stream_key, shape, shards, -0.22, 0.18) * entries
    return jnp.clip(entries, min=-most, max=most).astype(kind)


def heavy_noise(own_key, extent, spread, most, cuts, heavy, kind=jnp.bfloat16):
    entries = spread * jax.random.normal(own_key, extent, jnp.float32)
    if cuts:
        entries = entries * steps_of(own_key, extent, cuts, -0.22, 0.18)
    return jnp.clip(strengthened(entries, jax.random.fold_in(own_key, 3), *heavy), -most, most).astype(kind)


def setup_inputs(seed: int = 0) -> dict:
    streams_of = jax.random.split(jax.random.key(seed), 8)
    hidden_now = centred(streams_of[0], (TOKENS, D), 1.0, 6.0, ((0, 8),))
    hidden_next = draw_hidden_next(jax.random.fold_in(streams_of[7], 71), 0)
    cotangent = heavy_noise(streams_of[2], (TOKENS, VOCAB), 1.0, 6.0, ((0, 8), (1, 32)), (0, 1, 32, 2.75))
    master = draw_master(jax.random.fold_in(streams_of[7], 71), 0)
    moment = draw_moment(jax.random.fold_in(streams_of[7], 71), 0)
    second = draw_second(jax.random.fold_in(streams_of[7], 71), 0)
    targets = with_ends(jax.random.randint(streams_of[6], (TOKENS,), 0, VOCAB), jax.random.fold_in(streams_of[6], 1), 0, VOCAB - 1).astype(jnp.int32)
    return dict(hidden_now=hidden_now, hidden_next=hidden_next, cotangent=cotangent, master=master, moment=moment, second=second, targets=targets)


learn_rate = 0.02
beta_one = 0.9
beta_two = 0.95
epsilon = 1e-08
decay_rate = 0.1

def reference(hidden_now, hidden_next, cotangent, master, moment, second, targets):
    states = hidden_now.reshape(N_DP, TOK_GRP, D).astype(jnp.float32)
    blocks = jnp.transpose(cotangent.reshape(TOKENS, N_VOCAB, VS), (1, 0, 2))

    def update_block(pieces):
        master_b, moment_b, second_b, cot_b = pieces
        columns = cot_b.reshape(N_DP, TOK_GRP, VS).astype(jnp.float32)
        partial_value = jnp.einsum('gtv,gtd->gvd', columns, states)
        rounded = lax.optimization_barrier(partial_value.astype(jnp.bfloat16))
        gradient = lax.optimization_barrier(jnp.sum(rounded.astype(jnp.float32), axis=0))
        moment_new = beta_one * moment_b.astype(jnp.float32) + (1.0 - beta_one) * gradient
        second_new = beta_two * second_b.astype(jnp.float32) + (1.0 - beta_two) * gradient * gradient
        master_new = master_b - learn_rate * (moment_new / (jnp.sqrt(second_new) + epsilon) + decay_rate * master_b)
        return master_new.astype(jnp.bfloat16)
    head = lax.map(update_block, (master.reshape(N_VOCAB, VS, D), moment.reshape(N_VOCAB, VS, D), second.reshape(N_VOCAB, VS, D), blocks))
    head_rows = head.reshape(VOCAB, D)
    logits = jnp.dot(hidden_next, head_rows.T, preferred_element_type=jnp.float32)
    row_top = lax.optimization_barrier(jnp.max(logits, axis=1))
    row_total = lax.optimization_barrier(jnp.sum(jnp.exp(logits - row_top[:, None]), axis=1))
    picked = jnp.take_along_axis(logits, targets.astype(jnp.int32)[:, None], axis=1)[:, 0]
    row_loss = jnp.log(row_total) + row_top - picked
    return (logits.astype(jnp.bfloat16), row_loss)
```

```python
import jax
import jax.numpy as jnp
from jax import lax
from jax.experimental import pallas as pl
from jax.experimental.pallas import tpu as pltpu
from jax.sharding import PartitionSpec as P

learn_rate = 0.02
beta_one = 0.9
beta_two = 0.95
epsilon = 1e-08
decay_rate = 0.1

NX, NZL, NY, NZH, NC = 4, 2, 4, 4, 2
N_DP, N_VOCAB = NX * NZL, NY * NZH * NC
TOK = 128
HALF = TOK // 2
Q = HALF // 2
ROWS = 320
BLOCK = 512
BF16 = jnp.bfloat16
F32 = jnp.float32


def device_number(zl, x, y, zh, core):
    return (zl * NX + x) * N_VOCAB + (y * NZH + zh) * NC + core


def shift_pairs(dx, dz, flip):
    pairs = []
    for zl in range(NZL):
        for x in range(NX):
            for y in range(NY):
                for zh in range(NZH):
                    for core in range(NC):
                        z = (zh * 2 + zl + dz) % 8
                        source = device_number(z % 2, (x + dx) % NX, y, z // 2, core ^ flip)
                        pairs.append((source, device_number(zl, x, y, zh, core)))
    return pairs


def receive(value, dx=0, dz=0, flip=0):
    return lax.ppermute(value, ("dp", "vocab"), shift_pairs(dx, dz, flip))


A, B = 0, 1
LAYOUT = (
    (0, 1, A, 0, HALF), (HALF, 1, B, 0, HALF),
    (2 * HALF, 3, A, 0, HALF), (3 * HALF, 3, B, 0, HALF),
    (4 * HALF, 4, A, 0, HALF), (5 * HALF, 4, B, 0, HALF),
    (6 * HALF, 2, A, 0, HALF), (7 * HALF, 5, A, 0, Q),
    (7 * HALF + Q, 2, B, 0, HALF), (8 * HALF + Q, 7, B, Q, Q),
    (9 * HALF, 5, A, Q, Q), (9 * HALF + Q, 5, B, 0, HALF),
    (10 * HALF + Q, 7, A, 0, HALF), (11 * HALF + Q, 7, B, 0, Q),
    (12 * HALF, 6, A, 0, Q), (12 * HALF + Q, 6, B, Q, Q),
    (13 * HALF, 6, A, Q, Q), (13 * HALF + Q, 6, B, 0, Q),
)


def gather(hidden_now, hidden_next, core):
    start = core * HALF
    own = jnp.concatenate(
        [lax.dynamic_slice_in_dim(v, start, HALF, 0) for v in (hidden_now, hidden_next)], axis=0
    )
    a1, a2 = receive(own, dx=1), receive(own, dx=-1)
    b1, b2 = receive(own[:HALF], dz=1), receive(own[HALF:], dz=-1)
    r1 = receive(jnp.concatenate([a1, a2, b1, b2], axis=0), flip=1)
    c1 = receive(jnp.concatenate([a1[:HALF], b1[:Q]], axis=0), dx=1)
    c2 = receive(jnp.concatenate([a2[HALF:], b2[Q:]], axis=0), dx=-1)
    d1, d2 = receive(a1[Q:], dz=1), receive(a2[: 3 * Q], dz=-1)
    r2 = receive(jnp.concatenate([c1, c2, d1, d2], axis=0), flip=1)
    e1, e2 = receive(c1[HALF:], dx=1), receive(c2[HALF:], dx=-1)
    e3, e4 = receive(c1[Q:HALF], dz=1), receive(c2[:Q], dz=-1)
    r3 = receive(jnp.concatenate([e1, e2, e3, e4], axis=0), flip=1)
    return [a1, a2, b1, b2, c1, c2, d1, d2, e1, e2, e3, e4], [r1, r2, r3]


def plan(pieces):
    bounds = []
    at = 0
    for number, piece in enumerate(pieces):
        bounds.append((at, at + piece.shape[0], number))
        at += piece.shape[0]
    out = []
    for first, rank, array, row, rows in LAYOUT:
        (begin, number), = [(b, n) for b, e, n in bounds if b <= first and first + rows <= e]
        out.append((number, first - begin, rank, array, row, rows))
    return out


def update_kernel(mine, other, n_mine, place, now_ref, next_ref, *refs):
    n = n_mine + 3
    pieces, (cot_ref, master_ref, moment_ref, second_ref, out_ref, cot_t, blocks, total) = refs[:n], refs[n:]
    step = pl.program_id(0)

    @pl.when(step == 0)
    def _():
        for g in range(N_DP):
            cot_t[:, g * TOK : (g + 1) * TOK] = cot_ref[g]
        total[...] = jnp.zeros_like(total)

    for array, ref in ((A, now_ref), (B, next_ref)):
        blocks[array, pl.ds(pl.multiple_of(place[0], TOK), TOK), :] = ref[...]
    for table, first_ref, core_at in ((mine, 0, 8), (other, n_mine, 9)):
        for number, first, rank, array, row, rows in table:
            at = pl.multiple_of(place[rank] + place[core_at] + row, Q)
            blocks[array, pl.ds(at, rows), :] = pieces[first_ref + number][first : first + rows, :]

    gradient = jnp.dot(cot_t[...], blocks[A], preferred_element_type=F32)
    moment_new = beta_one * moment_ref[...].astype(F32) + (1.0 - beta_one) * gradient
    second_new = beta_two * second_ref[...].astype(F32) + (1.0 - beta_two) * gradient * gradient
    master = master_ref[...]
    rows_new = master - learn_rate * (moment_new / (jnp.sqrt(second_new) + epsilon) + decay_rate * master)
    total[...] += lax.dot_general(
        rows_new.astype(BF16), blocks[B], (((1,), (1,)), ((), ())), preferred_element_type=F32
    )

    @pl.when(step == pl.num_programs(0) - 1)
    def _():
        for g in range(N_DP):
            out_ref[g] = total[:, g * TOK : (g + 1) * TOK].astype(BF16)


def update_and_logits(place, hidden_now, hidden_next, mine, other, cot, master, moment, second):
    width = master.shape[1]
    column = lambda rows: pl.BlockSpec((rows, BLOCK), lambda j, place: (0, j))
    whole = pl.BlockSpec((N_DP, ROWS, TOK), lambda j, place: (0, 0, 0))
    pieces = list(mine) + list(other)
    kernel = lambda *refs: update_kernel(plan(mine), plan(other), len(mine), *refs)
    return pl.pallas_call(
        kernel,
        out_shape=jax.ShapeDtypeStruct((N_DP, ROWS, TOK), BF16),
        grid_spec=pltpu.PrefetchScalarGridSpec(
            num_scalar_prefetch=1,
            grid=(width // BLOCK,),
            in_specs=[column(TOK), column(TOK)]
            + [column(p.shape[0]) for p in pieces]
            + [whole, column(ROWS), column(ROWS), column(ROWS)],
            out_specs=whole,
            scratch_shapes=[
                pltpu.VMEM((ROWS, N_DP * TOK), BF16),
                pltpu.VMEM((2, N_DP * TOK, BLOCK), BF16),
                pltpu.VMEM((ROWS, N_DP * TOK), F32),
            ],
        ),
        compiler_params=pltpu.CompilerParams(vmem_limit_bytes=32 * 2**20),
        cost_estimate=pl.CostEstimate(flops=9_400_000_000, bytes_accessed=24_000_000, transcendentals=2_300_000),
        name="update_and_logits",
    )(place, hidden_now, hidden_next, *pieces, cot, master, moment, second)


def stats_kernel(logits_ref, target_ref, out_ref, stat_ref):
    value = logits_ref[...]
    wide = value.astype(F32)
    top = jnp.max(wide, axis=0, keepdims=True)
    sums = jnp.sum(jnp.exp(wide - top), axis=0, keepdims=True)
    positions = lax.broadcasted_iota(jnp.int32, wide.shape, 0)
    picked = jnp.sum(jnp.where(positions == target_ref[...], wide, 0.0), axis=0, keepdims=True)
    stats = jnp.concatenate([top, sums, picked], axis=0)
    stat_ref[...] = jnp.broadcast_to(stats[None], stat_ref.shape)
    out_ref[...] = value.T


def stats(logits_t, local_target):
    return pl.pallas_call(
        stats_kernel,
        out_shape=(
            jax.ShapeDtypeStruct((TOK, N_DP * ROWS), BF16),
            jax.ShapeDtypeStruct((N_VOCAB, 3, TOK), F32),
        ),
        name="stats",
    )(logits_t, local_target)


def loss_kernel(stat_ref, out_ref):
    value = stat_ref[...]
    top, sums, picked = value[:, 0], value[:, 1], value[:, 2]
    row_top = jnp.max(top, axis=0, keepdims=True)
    row_total = jnp.sum(sums * jnp.exp(top - row_top), axis=0, keepdims=True)
    out_ref[...] = jnp.log(row_total) + row_top - jnp.sum(picked, axis=0, keepdims=True)


def loss(stat):
    out = pl.pallas_call(
        loss_kernel, out_shape=jax.ShapeDtypeStruct((1, TOK), F32), name="loss"
    )(stat)
    return out.reshape(TOK)


def shards(hidden_now, hidden_next, cotangent, master, moment, second, targets):
    dp, vocab = lax.axis_index("dp"), lax.axis_index("vocab")
    core = vocab % NC
    ranks = [(((dp // NX + r // NX) % NZL) * NX + (dp + r % NX) % NX) * TOK for r in range(N_DP)]
    place = jnp.stack([r.astype(jnp.int32) for r in ranks + [core * HALF, (1 - core) * HALF]])
    cot = lax.all_to_all(cotangent.T.reshape(N_DP, ROWS, TOK), "dp", 0, 0)
    mine, other = gather(hidden_now, hidden_next, core)
    logits = update_and_logits(place, hidden_now, hidden_next, mine, other, cot, master, moment, second)
    logits = lax.all_to_all(logits, "dp", 0, 0).reshape(N_DP * ROWS, TOK)
    local_target = (targets - vocab * (N_DP * ROWS)).reshape(1, TOK)
    next_logits, stat = stats(logits, local_target)
    return next_logits, loss(lax.all_to_all(stat, "vocab", 0, 0))


def solution(mesh):
    in_specs = (
        P("dp", None),
        P("dp", None),
        P("dp", "vocab"),
        P(("vocab", "dp"), None),
        P(("vocab", "dp"), None),
        P(("vocab", "dp"), None),
        P("dp"),
    )
    out_specs = (P("dp", "vocab"), P("dp"))
    return jax.shard_map(shards, mesh=mesh, in_specs=in_specs, out_specs=out_specs, check_vma=False)
```

```python
import functools

import jax
import jax.numpy as jnp
from jax import lax
from jax.experimental import pallas as pl
from jax.experimental.pallas import tpu as pltpu
from jax.sharding import PartitionSpec as P

learn_rate = 0.02
beta_one = 0.9
beta_two = 0.95
epsilon = 1e-08
decay_rate = 0.1

NX, NZL, NY, NZH, NC = 4, 2, 4, 4, 2
NZ = NZL * NZH
N_DP, N_VOCAB = NX * NZL, NY * NZH * NC
TOK = 128
HALF = TOK // 2
CHUNK = 16
ROWS = 320
BLOCK = 512
MIB = 2**20
BF16 = jnp.bfloat16
F32 = jnp.float32


def device_number(x, y, z, core):
    return ((z % NZL) * NX + x) * N_VOCAB + (y * NZH + z // NZL) * NC + core


def receive(value, axes):
    pairs = []
    for x in range(NX):
        for y in range(NY):
            for z in range(NZ):
                for core in range(NC):
                    step = 1 - 2 * core
                    if axes == "core":
                        source = device_number(x, y, z, 1 - core)
                    else:
                        dx, dy, dz = (step if axis in axes else 0 for axis in "xyz")
                        source = device_number((x + dx) % NX, (y + dy) % NY, (z + dz) % NZ, core)
                    pairs.append((source, device_number(x, y, z, core)))
    return lax.ppermute(value, ("dp", "vocab"), pairs)


FIRST, SECOND = 0, 1
OWN, OTHER = 0, 1
HERE, SIDE, ACROSS = 0, 1, 2
CONTENTS = (
    ((0, SIDE, FIRST, OWN), (0, SIDE, FIRST, OTHER)),
    ((1, HERE, FIRST, OWN), (1, HERE, SECOND, OWN)),
    ((0, SIDE, SECOND, OWN), (0, SIDE, SECOND, OTHER)),
    ((1, SIDE, FIRST, OWN), (1, SIDE, FIRST, OTHER)),
    ((0, ACROSS, FIRST, OWN), (1, SIDE, SECOND, OWN)),
    ((0, ACROSS, SECOND, OWN), (1, SIDE, SECOND, OTHER)),
    ((1, ACROSS, FIRST, OWN),),
    ((1, ACROSS, SECOND, OWN),),
)


def pinned(value):
    return pltpu.with_memory_space_constraint(value, pltpu.VMEM)


def in_hbm(value):
    return pltpu.with_memory_space_constraint(value, pltpu.HBM)


VMEM = pl.BlockSpec(memory_space=pltpu.VMEM)
SMEM = pl.BlockSpec(memory_space=pltpu.SMEM)
HBM = pl.BlockSpec(memory_space=pltpu.HBM)
ANY = pl.BlockSpec(memory_space=pl.ANY)


def copy_rows(copies, sem):
    started = []
    for source, at, target, to in copies:
        for row in range(0, HALF, CHUNK):
            started.append(
                pltpu.make_async_copy(
                    source.at[pl.ds(pl.multiple_of(at + row, CHUNK), CHUNK)],
                    target.at[pl.ds(to + row, CHUNK)],
                    sem.at[len(started)],
                )
            )
    for each in started:
        each.start()
    for each in started:
        each.wait()


LATE = (False, False, False, False, False, True, True, True)


def arrange_kernel(place, now_ref, next_ref, x_ref, z_ref, sem):
    core, odd = place[0], place[1]
    own, other = core * HALF, (1 - core) * HALF

    def copy(first_ref, second_ref):
        copy_rows(
            (
                (first_ref, own, x_ref, 0),
                (first_ref, other, x_ref, HALF),
                (first_ref, own, z_ref, 0),
                (second_ref, own, z_ref, HALF),
            ),
            sem,
        )

    @pl.when(odd == 0)
    def _():
        copy(now_ref, next_ref)

    @pl.when(odd == 1)
    def _():
        copy(next_ref, now_ref)


def arrange(place, hidden_now, hidden_next):
    return pl.pallas_call(
        arrange_kernel,
        out_shape=(pltpu.VMEM(hidden_now.shape, BF16),) * 2,
        in_specs=[SMEM, HBM, HBM],
        out_specs=(VMEM,) * 2,
        scratch_shapes=[pltpu.SemaphoreType.DMA((4 * HALF // CHUNK,))],
        compiler_params=pltpu.CompilerParams(vmem_limit_bytes=4 * MIB),
        name="arrange",
    )(place, in_hbm(hidden_now), in_hbm(hidden_next))


EXTRA = 16


def prepare_kernel(cot_ref, target_ref, out_ref):
    turned = cot_ref[...].T
    target = target_ref[...]
    digits = [target // 16384, (target // 128) % 128, target % 128]
    rows = jnp.concatenate(digits + [jnp.zeros((EXTRA - 3, TOK), jnp.int32)], axis=0)
    rows = rows.astype(F32).astype(BF16)
    for g in range(N_DP):
        out_ref[g, :ROWS] = turned[g * ROWS : (g + 1) * ROWS]
        out_ref[g, ROWS:] = rows


def prepare(cotangent, targets):
    return pl.pallas_call(
        prepare_kernel,
        out_shape=jax.ShapeDtypeStruct((N_DP, ROWS + EXTRA, TOK), BF16),
        in_specs=[VMEM, VMEM],
        out_specs=VMEM,
        compiler_params=pltpu.CompilerParams(vmem_limit_bytes=2 * MIB),
        name="prepare",
    )(cotangent, targets.reshape(1, TOK))


def second_round_kernel(x1_ref, z1_ref, x_ref, sem):
    copy_rows(((x1_ref, 0, x_ref, 0), (z1_ref, HALF, x_ref, HALF)), sem)


def third_round_kernel(x2_ref, z2_ref, x_ref, y_ref, z_ref, sem):
    copy_rows(
        ((x2_ref, HALF, x_ref, 0), (x2_ref, 0, y_ref, 0), (z2_ref, HALF, y_ref, HALF), (x2_ref, 0, z_ref, 0)), sem
    )


def rearranged(kernel, values, rows):
    return pl.pallas_call(
        kernel,
        out_shape=tuple(pltpu.VMEM((n, values[0].shape[1]), BF16) for n in rows),
        in_specs=[ANY] * len(values),
        out_specs=(VMEM,) * len(rows),
        scratch_shapes=[pltpu.SemaphoreType.DMA((sum(rows) // CHUNK,))],
        compiler_params=pltpu.CompilerParams(vmem_limit_bytes=2 * MIB),
        name="rearranged",
    )(*values)


def gather(to_x, to_z, cot):
    swap = lambda v: receive(v, "core")
    x1, z1 = receive(to_x, "x"), receive(to_z, "z")
    cot, _, _ = lax.optimization_barrier((cot, x1, z1))
    cot = lax.all_to_all(cot, "dp", 0, 0)
    y2, z2 = receive(x1, "y"), receive(x1, "z")
    (to_x,) = rearranged(second_round_kernel, (x1, z1), (TOK,))
    x2 = receive(to_x, "x")
    y2, z2, x2, cot = lax.optimization_barrier((y2, z2, x2, cot))
    to_x, to_y, to_z = rearranged(third_round_kernel, (x2, z2), (HALF, TOK, HALF))
    y3, z3, x3 = receive(to_y, "y"), receive(to_z, "z"), receive(to_x, "x")
    mine = [x1, z1, y2, z2, x2, y3, z3, x3]
    return mine, [swap(v) for v in mine], cot


def update_kernel(place, now_ref, next_ref, *refs):
    n = 2 * len(CONTENTS)
    pieces, (cot_ref, *state), (out_ref, cot_t, hidden, *kept, total, sems) = refs[:n], refs[n : n + 4], refs[n + 4 :]
    steps = kept[0].shape[1] // BLOCK
    core, odd, dp, vocab = place[0], place[1], place[2], place[3]
    zl, x = dp // NX, lax.rem(dp, NX)
    rank_of = lambda dz, dx: (lax.rem(zl + dz, NZL)) * NX + lax.rem(x + dx, NX)

    copies = [(now_ref, 0, 0, dp * TOK, TOK), (next_ref, 0, 1, dp * TOK, TOK)]
    for group, half in ((0, core), (1, 1 - core)):
        x_at = (0, 1 + 2 * half, 2)
        for number, contents in enumerate(CONTENTS):
            for part, (dz, dx, array, which) in enumerate(contents):
                token = rank_of(dz, x_at[dx]) * TOK + (1 - half if which == OTHER else half) * HALF
                ref = pieces[group * len(CONTENTS) + number]
                copies.append((ref, part * HALF, 1 - odd if array == SECOND else odd, token, HALF))
    columns = lambda step: pl.ds(step * BLOCK, BLOCK)

    for step in range(steps):
        for ref, row, array, token, rows in copies:
            pltpu.make_async_copy(
                ref.at[pl.ds(row, rows), columns(step)],
                hidden.at[array, pl.ds(pl.multiple_of(token, HALF), rows), columns(step)],
                sems.at[step],
            ).start()
        for source, target in zip(state, kept):
            pltpu.make_async_copy(source.at[:, columns(step)], target.at[:, columns(step)], sems.at[step]).start()

    for g in range(N_DP):
        cot_t[:, g * TOK : (g + 1) * TOK] = cot_ref[g, :ROWS]
    for step in range(steps):
        now = hidden.at[:, :, columns(step)]
        pltpu.make_async_copy(now, now, sems.at[step]).wait()
        for target in kept:
            now = target.at[:, columns(step)]
            pltpu.make_async_copy(now, now, sems.at[step]).wait()
        gradient = jnp.dot(cot_t[...], hidden[0, :, columns(step)], preferred_element_type=F32)
        master, moment, second = (target[:, columns(step)].astype(F32) for target in kept)
        moment_new = beta_one * moment + (1.0 - beta_one) * gradient
        second_new = beta_two * second + (1.0 - beta_two) * gradient * gradient
        rows_new = master - learn_rate * (moment_new / (jnp.sqrt(second_new) + epsilon) + decay_rate * master)
        product = lax.dot_general(
            rows_new.astype(BF16), hidden[1, :, columns(step)], (((1,), (1,)), ((), ())), preferred_element_type=F32
        )
        if step == 0:
            total[...] = product
        else:
            total[...] += product

    first_row = vocab * (N_DP * ROWS) + dp * ROWS
    positions = lax.broadcasted_iota(jnp.int32, (ROWS, TOK), 0) + first_row
    for g in range(N_DP):
        logits = total[:, g * TOK : (g + 1) * TOK]
        digits = cot_ref[g, ROWS : ROWS + 3].astype(F32)
        target = (digits[0:1] * 16384.0 + digits[1:2] * 128.0 + digits[2:3]).astype(jnp.int32)
        top = jnp.max(logits, axis=0, keepdims=True)
        sums = jnp.sum(jnp.exp(logits - top), axis=0, keepdims=True)
        picked = jnp.sum(jnp.where(positions == target, logits, 0.0), axis=0, keepdims=True)
        rest = jnp.concatenate([top, sums, picked], axis=0)
        rows = []
        for _ in range(3):
            rows.append(rest.astype(BF16).astype(F32))
            rest = rest - rows[-1]
        rows.append(jnp.zeros((EXTRA - 9, TOK), F32))
        out_ref[g, :ROWS] = logits.astype(BF16)
        out_ref[g, ROWS:] = jnp.concatenate(rows, axis=0).astype(BF16)


def update_and_logits(place, now_next, mine, other, cot, state):
    whole = (N_DP, ROWS + EXTRA, TOK)
    placed = [pinned(v) if late else in_hbm(v) for values in (mine, other) for v, late in zip(values, LATE)]
    width = state[0].shape[1]
    return pl.pallas_call(
        update_kernel,
        out_shape=jax.ShapeDtypeStruct(whole, BF16),
        in_specs=[SMEM, HBM, HBM] + [ANY] * (len(mine) + len(other)) + [VMEM] + [HBM] * 3,
        out_specs=VMEM,
        scratch_shapes=[
            pltpu.VMEM((ROWS, N_DP * TOK), BF16),
            pltpu.VMEM((2, N_DP * TOK, width), BF16),
            *[pltpu.VMEM(v.shape, v.dtype) for v in state],
            pltpu.VMEM((ROWS, N_DP * TOK), F32),
            pltpu.SemaphoreType.DMA((width // BLOCK,)),
        ],
        compiler_params=pltpu.CompilerParams(vmem_limit_bytes=32 * MIB),
        cost_estimate=pl.CostEstimate(flops=9_400_000_000, bytes_accessed=24_000_000, transcendentals=2_300_000),
        name="update_and_logits",
    )(place, *[in_hbm(v) for v in now_next], *placed, cot, *[in_hbm(v) for v in state])


def turn_kernel(part_ref, out_ref):
    rows = jnp.concatenate([part_ref[g, :ROWS] for g in range(N_DP)], axis=0)
    out_ref[...] = rows.T


def turn(parts):
    return pl.pallas_call(
        turn_kernel,
        out_shape=jax.ShapeDtypeStruct((TOK, N_DP * ROWS), BF16),
        in_specs=[VMEM],
        out_specs=VMEM,
        compiler_params=pltpu.CompilerParams(vmem_limit_bytes=4 * MIB),
        cost_estimate=pl.CostEstimate(flops=0, bytes_accessed=1_400_000, transcendentals=0),
        name="turn",
    )(parts)


def merged(value):
    top, sums, picked = value[:, 0], value[:, 1], value[:, 2]
    row_top = jnp.max(top, axis=0, keepdims=True)
    row_total = jnp.sum(sums * jnp.exp(top - row_top), axis=0, keepdims=True)
    return row_top, row_total, jnp.sum(picked, axis=0, keepdims=True)


def merge_kernel(part_ref, out_ref, extra, sem):
    load = pltpu.make_async_copy(part_ref.at[:, pl.ds(ROWS, EXTRA), :], extra, sem)
    load.start()
    load.wait()
    rows = extra[...].astype(F32)
    value = rows[:, 0:3] + rows[:, 3:6] + rows[:, 6:9]
    out_ref[...] = jnp.broadcast_to(jnp.concatenate(merged(value), axis=0)[None], out_ref.shape)


def merge(parts):
    return pl.pallas_call(
        merge_kernel,
        out_shape=jax.ShapeDtypeStruct((N_VOCAB, 3, TOK), F32),
        in_specs=[ANY],
        out_specs=VMEM,
        scratch_shapes=[pltpu.VMEM((N_DP, EXTRA, TOK), BF16), pltpu.SemaphoreType.DMA(())],
        compiler_params=pltpu.CompilerParams(vmem_limit_bytes=4 * MIB),
        name="merge",
    )(parts)


def loss_kernel(stat_ref, out_ref):
    row_top, row_total, picked = merged(stat_ref[...])
    out_ref[...] = jnp.log(row_total) + row_top - picked


def loss(stat):
    out = pl.pallas_call(
        loss_kernel,
        out_shape=jax.ShapeDtypeStruct((1, TOK), F32),
        in_specs=[VMEM],
        out_specs=VMEM,
        compiler_params=pltpu.CompilerParams(vmem_limit_bytes=4 * MIB),
        name="loss",
    )(stat)
    return out.reshape(TOK)


def shards(hidden_now, hidden_next, cotangent, master, moment, second, targets):
    dp, vocab = lax.axis_index("dp"), lax.axis_index("vocab")
    place = jnp.stack([vocab % NC, (vocab // (NZH * NC)) % 2, dp, vocab]).astype(jnp.int32)
    to_x, to_z = arrange(place, hidden_now, hidden_next)
    mine, other, cot = gather(to_x, to_z, prepare(cotangent, targets))
    parts = update_and_logits(place, (hidden_now, hidden_next), mine, other, cot, (master, moment, second))
    parts = lax.all_to_all(parts, "dp", 0, 0)
    stat = lax.all_to_all(merge(parts), "vocab", 0, 0)
    return turn(parts), loss(stat)


def solution(mesh):
    in_specs = (
        P("dp", None),
        P("dp", None),
        P("dp", "vocab"),
        P(("vocab", "dp"), None),
        P(("vocab", "dp"), None),
        P(("vocab", "dp"), None),
        P("dp"),
    )
    out_specs = (P("dp", "vocab"), P("dp"))
    return jax.shard_map(shards, mesh=mesh, in_specs=in_specs, out_specs=out_specs, check_vma=False)
```

```python
import functools

import jax
import jax.numpy as jnp
from jax import lax
from jax.experimental import pallas as pl
from jax.experimental.pallas import tpu as pltpu
from jax.sharding import PartitionSpec as P

learn_rate = 0.02
beta_one = 0.9
beta_two = 0.95
epsilon = 1e-08
decay_rate = 0.1

NX, NZL, NY, NZH, NC = 4, 2, 4, 4, 2
NZ = NZL * NZH
N_DP, N_VOCAB = NX * NZL, NY * NZH * NC
TOK = 128
HALF = TOK // 2
CHUNK = 16
ROWS = 320
BLOCK = 512
MIB = 2**20
BF16 = jnp.bfloat16
F32 = jnp.float32


def device_number(x, y, z, core):
    return ((z % NZL) * NX + x) * N_VOCAB + (y * NZH + z // NZL) * NC + core


def receive(value, axes):
    pairs = []
    for x in range(NX):
        for y in range(NY):
            for z in range(NZ):
                for core in range(NC):
                    step = 1 - 2 * core
                    if axes == "core":
                        source = device_number(x, y, z, 1 - core)
                    else:
                        dx, dy, dz = (step if axis in axes else 0 for axis in "xyz")
                        source = device_number((x + dx) % NX, (y + dy) % NY, (z + dz) % NZ, core)
                    pairs.append((source, device_number(x, y, z, core)))
    return lax.ppermute(value, ("dp", "vocab"), pairs)


FIRST, SECOND = 0, 1
OWN, OTHER = 0, 1
HERE, SIDE, ACROSS = 0, 1, 2
CONTENTS = (
    ((0, SIDE, FIRST, OWN), (0, SIDE, FIRST, OTHER)),
    ((1, HERE, FIRST, OWN), (1, HERE, SECOND, OWN)),
    ((0, SIDE, SECOND, OWN), (0, SIDE, SECOND, OTHER)),
    ((1, SIDE, FIRST, OWN), (1, SIDE, FIRST, OTHER)),
    ((0, ACROSS, FIRST, OWN), (1, SIDE, SECOND, OWN)),
    ((0, ACROSS, SECOND, OWN), (1, SIDE, SECOND, OTHER)),
    ((1, ACROSS, SECOND, OWN), (1, ACROSS, FIRST, OWN)),
)


def pinned(value):
    return pltpu.with_memory_space_constraint(value, pltpu.VMEM)


def in_hbm(value):
    return pltpu.with_memory_space_constraint(value, pltpu.HBM)


VMEM = pl.BlockSpec(memory_space=pltpu.VMEM)
SMEM = pl.BlockSpec(memory_space=pltpu.SMEM)
HBM = pl.BlockSpec(memory_space=pltpu.HBM)
ANY = pl.BlockSpec(memory_space=pl.ANY)


def copy_rows(copies, sem):
    started = []
    for source, at, target, to in copies:
        for row in range(0, HALF, CHUNK):
            started.append(
                pltpu.make_async_copy(
                    source.at[pl.ds(pl.multiple_of(at + row, CHUNK), CHUNK)],
                    target.at[pl.ds(to + row, CHUNK)],
                    sem.at[len(started)],
                )
            )
    for each in started:
        each.start()
    for each in started:
        each.wait()


LATE = (False, False, False, False, False, True, True)


def arrange_kernel(place, now_ref, next_ref, x_ref, z_ref, sem):
    core, odd = place[0], place[1]
    own, other = core * HALF, (1 - core) * HALF

    def copy(first_ref, second_ref):
        copy_rows(
            (
                (first_ref, own, x_ref, 0),
                (first_ref, other, x_ref, HALF),
                (first_ref, own, z_ref, 0),
                (second_ref, own, z_ref, HALF),
            ),
            sem,
        )

    @pl.when(odd == 0)
    def _():
        copy(now_ref, next_ref)

    @pl.when(odd == 1)
    def _():
        copy(next_ref, now_ref)


def arrange(place, hidden_now, hidden_next):
    return pl.pallas_call(
        arrange_kernel,
        out_shape=(pltpu.VMEM(hidden_now.shape, BF16),) * 2,
        in_specs=[SMEM, HBM, HBM],
        out_specs=(VMEM,) * 2,
        scratch_shapes=[pltpu.SemaphoreType.DMA((4 * HALF // CHUNK,))],
        compiler_params=pltpu.CompilerParams(vmem_limit_bytes=4 * MIB),
        name="arrange",
    )(place, in_hbm(hidden_now), in_hbm(hidden_next))


EXTRA = 16


def prepare_kernel(cot_ref, target_ref, out_ref):
    turned = cot_ref[...].T
    target = target_ref[...]
    digits = [target // 16384, (target // 128) % 128, target % 128]
    rows = jnp.concatenate(digits + [jnp.zeros((EXTRA - 3, TOK), jnp.int32)], axis=0)
    rows = rows.astype(F32).astype(BF16)
    for g in range(N_DP):
        out_ref[g, :ROWS] = turned[g * ROWS : (g + 1) * ROWS]
        out_ref[g, ROWS:] = rows


def prepare(cotangent, targets):
    return pl.pallas_call(
        prepare_kernel,
        out_shape=jax.ShapeDtypeStruct((N_DP, ROWS + EXTRA, TOK), BF16),
        in_specs=[VMEM, VMEM],
        out_specs=VMEM,
        compiler_params=pltpu.CompilerParams(vmem_limit_bytes=2 * MIB),
        name="prepare",
    )(cotangent, targets.reshape(1, TOK))


def second_round_kernel(x1_ref, z1_ref, x_ref, sem):
    load = pltpu.make_async_copy(z1_ref.at[pl.ds(HALF, HALF)], x_ref.at[pl.ds(HALF, HALF)], sem)
    load.start()
    x_ref[:HALF] = x1_ref[:HALF]
    load.wait()


def third_round_kernel(x2_ref, z2_ref, x_ref, y_ref):
    x_ref[:HALF] = x2_ref[HALF:]
    x_ref[HALF:] = z2_ref[:HALF]
    y_ref[:HALF] = x2_ref[:HALF]
    y_ref[HALF:] = z2_ref[HALF:]


def rearranged(kernel, values, outputs, in_specs, scratch=()):
    return pl.pallas_call(
        kernel,
        out_shape=(pltpu.VMEM(values[0].shape, BF16),) * outputs,
        in_specs=in_specs,
        out_specs=(VMEM,) * outputs,
        scratch_shapes=scratch,
        compiler_params=pltpu.CompilerParams(vmem_limit_bytes=4 * MIB),
        name="rearranged",
    )(*values)


def gather(to_x, to_z, cot):
    swap = lambda v: receive(v, "core")
    x1, z1 = receive(to_x, "x"), receive(to_z, "z")
    cot, _, _ = lax.optimization_barrier((cot, x1, z1))
    cot = lax.all_to_all(cot, "dp", 0, 0)
    y2, z2 = receive(x1, "y"), receive(x1, "z")
    (to_x,) = rearranged(
        second_round_kernel, (pinned(x1), z1), 1, [VMEM, ANY], [pltpu.SemaphoreType.DMA(())]
    )
    x2 = receive(to_x, "x")
    y2, z2, x2, cot = lax.optimization_barrier((y2, z2, x2, cot))
    to_x, to_y = rearranged(third_round_kernel, (pinned(x2), pinned(z2)), 2, [VMEM, VMEM])
    y3, x3 = receive(to_y, "y"), receive(to_x, "x")
    mine = [x1, z1, y2, z2, x2, y3, x3]
    return mine, [swap(v) for v in mine], cot


def update_kernel(place, now_ref, next_ref, *refs):
    n = 2 * len(CONTENTS)
    pieces, (cot_ref, *state), (out_ref, cot_t, hidden, *kept, total, sems) = refs[:n], refs[n : n + 4], refs[n + 4 :]
    steps = kept[0].shape[1] // BLOCK
    core, odd, dp, vocab = place[0], place[1], place[2], place[3]
    zl, x = dp // NX, lax.rem(dp, NX)
    rank_of = lambda dz, dx: (lax.rem(zl + dz, NZL)) * NX + lax.rem(x + dx, NX)

    copies = [(now_ref, 0, 0, dp * TOK, TOK), (next_ref, 0, 1, dp * TOK, TOK)]
    for group, half in ((0, core), (1, 1 - core)):
        x_at = (0, 1 + 2 * half, 2)
        for number, contents in enumerate(CONTENTS):
            for part, (dz, dx, array, which) in enumerate(contents):
                token = rank_of(dz, x_at[dx]) * TOK + (1 - half if which == OTHER else half) * HALF
                ref = pieces[group * len(CONTENTS) + number]
                copies.append((ref, part * HALF, 1 - odd if array == SECOND else odd, token, HALF))
    columns = lambda step: pl.ds(step * BLOCK, BLOCK)

    for step in range(steps):
        for ref, row, array, token, rows in copies:
            pltpu.make_async_copy(
                ref.at[pl.ds(row, rows), columns(step)],
                hidden.at[array, pl.ds(pl.multiple_of(token, HALF), rows), columns(step)],
                sems.at[step],
            ).start()
        for source, target in zip(state, kept):
            pltpu.make_async_copy(source.at[:, columns(step)], target.at[:, columns(step)], sems.at[step]).start()

    for g in range(N_DP):
        cot_t[:, g * TOK : (g + 1) * TOK] = cot_ref[g, :ROWS]
    for step in range(steps):
        now = hidden.at[:, :, columns(step)]
        pltpu.make_async_copy(now, now, sems.at[step]).wait()
        for target in kept:
            now = target.at[:, columns(step)]
            pltpu.make_async_copy(now, now, sems.at[step]).wait()
        gradient = jnp.dot(cot_t[...], hidden[0, :, columns(step)], preferred_element_type=F32)
        master, moment, second = (target[:, columns(step)].astype(F32) for target in kept)
        moment_new = beta_one * moment + (1.0 - beta_one) * gradient
        second_new = beta_two * second + (1.0 - beta_two) * gradient * gradient
        rows_new = master - learn_rate * (moment_new / (jnp.sqrt(second_new) + epsilon) + decay_rate * master)
        product = lax.dot_general(
            rows_new.astype(BF16), hidden[1, :, columns(step)], (((1,), (1,)), ((), ())), preferred_element_type=F32
        )
        if step == 0:
            total[...] = product
        else:
            total[...] += product

    first_row = vocab * (N_DP * ROWS) + dp * ROWS
    positions = lax.broadcasted_iota(jnp.int32, (ROWS, TOK), 0) + first_row
    for g in range(N_DP):
        logits = total[:, g * TOK : (g + 1) * TOK]
        digits = cot_ref[g, ROWS : ROWS + 3].astype(F32)
        target = (digits[0:1] * 16384.0 + digits[1:2] * 128.0 + digits[2:3]).astype(jnp.int32)
        top = jnp.max(logits, axis=0, keepdims=True)
        sums = jnp.sum(jnp.exp(logits - top), axis=0, keepdims=True)
        picked = jnp.sum(jnp.where(positions == target, logits, 0.0), axis=0, keepdims=True)
        rest = jnp.concatenate([top, sums, picked], axis=0)
        rows = []
        for _ in range(3):
            rows.append(rest.astype(BF16).astype(F32))
            rest = rest - rows[-1]
        rows.append(jnp.zeros((EXTRA - 9, TOK), F32))
        out_ref[g, :ROWS] = logits.astype(BF16)
        out_ref[g, ROWS:] = jnp.concatenate(rows, axis=0).astype(BF16)


def update_and_logits(place, now_next, mine, other, cot, state):
    whole = (N_DP, ROWS + EXTRA, TOK)
    placed = [pinned(v) if late else in_hbm(v) for values in (mine, other) for v, late in zip(values, LATE)]
    width = state[0].shape[1]
    return pl.pallas_call(
        update_kernel,
        out_shape=jax.ShapeDtypeStruct(whole, BF16),
        in_specs=[SMEM, HBM, HBM] + [ANY] * (len(mine) + len(other)) + [VMEM] + [HBM] * 3,
        out_specs=VMEM,
        scratch_shapes=[
            pltpu.VMEM((ROWS, N_DP * TOK), BF16),
            pltpu.VMEM((2, N_DP * TOK, width), BF16),
            *[pltpu.VMEM(v.shape, v.dtype) for v in state],
            pltpu.VMEM((ROWS, N_DP * TOK), F32),
            pltpu.SemaphoreType.DMA((width // BLOCK,)),
        ],
        compiler_params=pltpu.CompilerParams(vmem_limit_bytes=32 * MIB),
        cost_estimate=pl.CostEstimate(flops=9_400_000_000, bytes_accessed=24_000_000, transcendentals=2_300_000),
        name="update_and_logits",
    )(place, *[in_hbm(v) for v in now_next], *placed, cot, *[in_hbm(v) for v in state])


def turn_kernel(part_ref, out_ref):
    rows = jnp.concatenate([part_ref[g, :ROWS] for g in range(N_DP)], axis=0)
    out_ref[...] = rows.T


def turn(parts):
    return pl.pallas_call(
        turn_kernel,
        out_shape=jax.ShapeDtypeStruct((TOK, N_DP * ROWS), BF16),
        in_specs=[VMEM],
        out_specs=VMEM,
        compiler_params=pltpu.CompilerParams(vmem_limit_bytes=4 * MIB),
        cost_estimate=pl.CostEstimate(flops=0, bytes_accessed=1_400_000, transcendentals=0),
        name="turn",
    )(parts)


def merged(value):
    top, sums, picked = value[:, 0], value[:, 1], value[:, 2]
    row_top = jnp.max(top, axis=0, keepdims=True)
    row_total = jnp.sum(sums * jnp.exp(top - row_top), axis=0, keepdims=True)
    return row_top, row_total, jnp.sum(picked, axis=0, keepdims=True)


def merge_kernel(part_ref, out_ref, extra, sem):
    load = pltpu.make_async_copy(part_ref.at[:, pl.ds(ROWS, EXTRA), :], extra, sem)
    load.start()
    load.wait()
    rows = extra[...].astype(F32)
    value = rows[:, 0:3] + rows[:, 3:6] + rows[:, 6:9]
    out_ref[...] = jnp.broadcast_to(jnp.concatenate(merged(value), axis=0)[None], out_ref.shape)


def merge(parts):
    return pl.pallas_call(
        merge_kernel,
        out_shape=jax.ShapeDtypeStruct((N_VOCAB, 3, TOK), F32),
        in_specs=[ANY],
        out_specs=VMEM,
        scratch_shapes=[pltpu.VMEM((N_DP, EXTRA, TOK), BF16), pltpu.SemaphoreType.DMA(())],
        compiler_params=pltpu.CompilerParams(vmem_limit_bytes=4 * MIB),
        name="merge",
    )(parts)


def loss_kernel(stat_ref, out_ref):
    row_top, row_total, picked = merged(stat_ref[...])
    out_ref[...] = jnp.log(row_total) + row_top - picked


def loss(stat):
    out = pl.pallas_call(
        loss_kernel,
        out_shape=jax.ShapeDtypeStruct((1, TOK), F32),
        in_specs=[VMEM],
        out_specs=VMEM,
        compiler_params=pltpu.CompilerParams(vmem_limit_bytes=4 * MIB),
        name="loss",
    )(stat)
    return out.reshape(TOK)


def shards(hidden_now, hidden_next, cotangent, master, moment, second, targets):
    dp, vocab = lax.axis_index("dp"), lax.axis_index("vocab")
    place = jnp.stack([vocab % NC, (vocab // (NZH * NC)) % 2, dp, vocab]).astype(jnp.int32)
    to_x, to_z = arrange(place, hidden_now, hidden_next)
    mine, other, cot = gather(to_x, to_z, prepare(cotangent, targets))
    parts = update_and_logits(place, (hidden_now, hidden_next), mine, other, cot, (master, moment, second))
    parts = lax.all_to_all(parts, "dp", 0, 0)
    stat = lax.all_to_all(merge(parts), "vocab", 0, 0)
    return turn(parts), loss(stat)


def solution(mesh):
    in_specs = (
        P("dp", None),
        P("dp", None),
        P("dp", "vocab"),
        P(("vocab", "dp"), None),
        P(("vocab", "dp"), None),
        P(("vocab", "dp"), None),
        P("dp"),
    )
    out_specs = (P("dp", "vocab"), P("dp"))
    return jax.shard_map(shards, mesh=mesh, in_specs=in_specs, out_specs=out_specs, check_vma=False)
```

```python
import functools

import jax
import jax.numpy as jnp
from jax import lax
from jax.experimental import pallas as pl
from jax.experimental.pallas import tpu as pltpu
from jax.sharding import PartitionSpec as P

learn_rate = 0.02
beta_one = 0.9
beta_two = 0.95
epsilon = 1e-08
decay_rate = 0.1

NX, NZL, NY, NZH, NC = 4, 2, 4, 4, 2
NZ = NZL * NZH
N_DP, N_VOCAB = NX * NZL, NY * NZH * NC
TOK = 128
HALF = TOK // 2
CHUNK = 16
ROWS = 320
BLOCK = 512
MIB = 2**20
BF16 = jnp.bfloat16
F32 = jnp.float32


def device_number(x, y, z, core):
    return ((z % NZL) * NX + x) * N_VOCAB + (y * NZH + z // NZL) * NC + core


def receive(value, axes):
    pairs = []
    for x in range(NX):
        for y in range(NY):
            for z in range(NZ):
                for core in range(NC):
                    step = 1 - 2 * core
                    if axes == "core":
                        source = device_number(x, y, z, 1 - core)
                    else:
                        dx, dy, dz = (step if axis in axes else 0 for axis in "xyz")
                        source = device_number((x + dx) % NX, (y + dy) % NY, (z + dz) % NZ, core)
                    pairs.append((source, device_number(x, y, z, core)))
    return lax.ppermute(value, ("dp", "vocab"), pairs)


FIRST, SECOND = 0, 1
OWN, OTHER = 0, 1
HERE, SIDE, ACROSS = 0, 1, 2
CONTENTS = (
    ((0, SIDE, FIRST, OWN), (0, SIDE, FIRST, OTHER)),
    ((1, HERE, FIRST, OWN), (1, HERE, SECOND, OWN)),
    ((0, SIDE, SECOND, OWN), (0, SIDE, SECOND, OTHER)),
    ((1, SIDE, FIRST, OWN), (1, SIDE, FIRST, OTHER)),
    ((0, ACROSS, FIRST, OWN), (1, SIDE, SECOND, OWN)),
    ((0, ACROSS, SECOND, OWN), (1, SIDE, SECOND, OTHER)),
    ((1, ACROSS, SECOND, OWN), (1, ACROSS, FIRST, OWN)),
)


def pinned(value):
    return pltpu.with_memory_space_constraint(value, pltpu.VMEM)


def in_hbm(value):
    return pltpu.with_memory_space_constraint(value, pltpu.HBM)


VMEM = pl.BlockSpec(memory_space=pltpu.VMEM)
SMEM = pl.BlockSpec(memory_space=pltpu.SMEM)
HBM = pl.BlockSpec(memory_space=pltpu.HBM)
ANY = pl.BlockSpec(memory_space=pl.ANY)


def copy_rows(copies, sem):
    started = []
    for source, at, target, to in copies:
        for row in range(0, HALF, CHUNK):
            started.append(
                pltpu.make_async_copy(
                    source.at[pl.ds(pl.multiple_of(at + row, CHUNK), CHUNK)],
                    target.at[pl.ds(to + row, CHUNK)],
                    sem.at[len(started)],
                )
            )
    for each in started:
        each.start()
    for each in started:
        each.wait()


LATE = (False, False, False, False, False, True, True)


def arrange_kernel(place, now_ref, next_ref, x_ref, z_ref, sem):
    core, odd = place[0], place[1]
    own, other = core * HALF, (1 - core) * HALF

    def copy(first_ref, second_ref):
        copy_rows(
            ((first_ref, own, x_ref, 0), (second_ref, own, z_ref, HALF), (first_ref, other, x_ref, HALF)), sem
        )
        z_ref[:HALF] = x_ref[:HALF]

    @pl.when(odd == 0)
    def _():
        copy(now_ref, next_ref)

    @pl.when(odd == 1)
    def _():
        copy(next_ref, now_ref)


def arrange(place, hidden_now, hidden_next):
    return pl.pallas_call(
        arrange_kernel,
        out_shape=(pltpu.VMEM(hidden_now.shape, BF16),) * 2,
        in_specs=[SMEM, HBM, HBM],
        out_specs=(VMEM,) * 2,
        scratch_shapes=[pltpu.SemaphoreType.DMA((4 * HALF // CHUNK,))],
        compiler_params=pltpu.CompilerParams(vmem_limit_bytes=4 * MIB),
        name="arrange",
    )(place, in_hbm(hidden_now), in_hbm(hidden_next))


EXTRA = 16


def prepare_kernel(cot_ref, target_ref, out_ref):
    turned = cot_ref[...].T
    target = target_ref[...]
    digits = [target // 16384, (target // 128) % 128, target % 128]
    rows = jnp.concatenate(digits + [jnp.zeros((EXTRA - 3, TOK), jnp.int32)], axis=0)
    rows = rows.astype(F32).astype(BF16)
    for g in range(N_DP):
        out_ref[g, :ROWS] = turned[g * ROWS : (g + 1) * ROWS]
        out_ref[g, ROWS:] = rows


def prepare(cotangent, targets):
    return pl.pallas_call(
        prepare_kernel,
        out_shape=jax.ShapeDtypeStruct((N_DP, ROWS + EXTRA, TOK), BF16),
        in_specs=[VMEM, VMEM],
        out_specs=VMEM,
        compiler_params=pltpu.CompilerParams(vmem_limit_bytes=2 * MIB),
        name="prepare",
    )(cotangent, targets.reshape(1, TOK))


def second_round_kernel(x1_ref, z1_ref, x_ref, sem):
    load = pltpu.make_async_copy(z1_ref.at[pl.ds(HALF, HALF)], x_ref.at[pl.ds(HALF, HALF)], sem)
    load.start()
    x_ref[:HALF] = x1_ref[:HALF]
    load.wait()


def third_round_kernel(x2_ref, z2_ref, x_ref, y_ref):
    x_ref[:HALF] = x2_ref[HALF:]
    x_ref[HALF:] = z2_ref[:HALF]
    y_ref[:HALF] = x2_ref[:HALF]
    y_ref[HALF:] = z2_ref[HALF:]


def rearranged(kernel, values, outputs, in_specs, scratch=()):
    return pl.pallas_call(
        kernel,
        out_shape=(pltpu.VMEM(values[0].shape, BF16),) * outputs,
        in_specs=in_specs,
        out_specs=(VMEM,) * outputs,
        scratch_shapes=scratch,
        compiler_params=pltpu.CompilerParams(vmem_limit_bytes=4 * MIB),
        name="rearranged",
    )(*values)


def gather(to_x, to_z, cot):
    swap = lambda v: receive(v, "core")
    x1, z1 = receive(to_x, "x"), receive(to_z, "z")
    cot, _ = lax.optimization_barrier((cot, x1))
    cot = lax.all_to_all(cot, "dp", 0, 0)
    y2, z2 = receive(x1, "y"), receive(x1, "z")
    (to_x,) = rearranged(
        second_round_kernel, (pinned(x1), z1), 1, [VMEM, ANY], [pltpu.SemaphoreType.DMA(())]
    )
    x2 = receive(to_x, "x")
    y2, z2, x2, cot = lax.optimization_barrier((y2, z2, x2, cot))
    to_x, to_y = rearranged(third_round_kernel, (pinned(x2), pinned(z2)), 2, [VMEM, VMEM])
    y3, x3 = receive(to_y, "y"), receive(to_x, "x")
    mine = [x1, z1, y2, z2, x2, y3, x3]
    return mine, [swap(v) for v in mine], cot


def update_kernel(place, now_ref, next_ref, *refs):
    n = 2 * len(CONTENTS)
    pieces, (cot_ref, *state), (out_ref, cot_t, hidden, *kept, total, sems) = refs[:n], refs[n : n + 4], refs[n + 4 :]
    steps = kept[0].shape[1] // BLOCK
    core, odd, dp, vocab = place[0], place[1], place[2], place[3]
    zl, x = dp // NX, lax.rem(dp, NX)
    rank_of = lambda dz, dx: (lax.rem(zl + dz, NZL)) * NX + lax.rem(x + dx, NX)

    copies = [(now_ref, 0, 0, dp * TOK, TOK), (next_ref, 0, 1, dp * TOK, TOK)]
    for group, half in ((0, core), (1, 1 - core)):
        x_at = (0, 1 + 2 * half, 2)
        for number, contents in enumerate(CONTENTS):
            for part, (dz, dx, array, which) in enumerate(contents):
                token = rank_of(dz, x_at[dx]) * TOK + (1 - half if which == OTHER else half) * HALF
                ref = pieces[group * len(CONTENTS) + number]
                copies.append((ref, part * HALF, 1 - odd if array == SECOND else odd, token, HALF))
    columns = lambda step: pl.ds(step * BLOCK, BLOCK)

    for step in range(steps):
        for ref, row, array, token, rows in copies:
            pltpu.make_async_copy(
                ref.at[pl.ds(row, rows), columns(step)],
                hidden.at[array, pl.ds(pl.multiple_of(token, HALF), rows), columns(step)],
                sems.at[step],
            ).start()
        for source, target in zip(state, kept):
            pltpu.make_async_copy(source.at[:, columns(step)], target.at[:, columns(step)], sems.at[step]).start()

    for g in range(N_DP):
        cot_t[:, g * TOK : (g + 1) * TOK] = cot_ref[g, :ROWS]
    for step in range(steps):
        now = hidden.at[:, :, columns(step)]
        pltpu.make_async_copy(now, now, sems.at[step]).wait()
        for target in kept:
            now = target.at[:, columns(step)]
            pltpu.make_async_copy(now, now, sems.at[step]).wait()
        gradient = jnp.dot(cot_t[...], hidden[0, :, columns(step)], preferred_element_type=F32)
        master, moment, second = (target[:, columns(step)].astype(F32) for target in kept)
        moment_new = beta_one * moment + (1.0 - beta_one) * gradient
        second_new = beta_two * second + (1.0 - beta_two) * gradient * gradient
        root = second_new * lax.rsqrt(second_new)
        scale = lax.rsqrt(second_new + epsilon * (2.0 * root + epsilon))
        rows_new = (1.0 - learn_rate * decay_rate) * master - learn_rate * (moment_new * scale)
        product = lax.dot_general(
            rows_new.astype(BF16), hidden[1, :, columns(step)], (((1,), (1,)), ((), ())), preferred_element_type=F32
        )
        if step == 0:
            total[...] = product
        else:
            total[...] += product

    first_row = vocab * (N_DP * ROWS) + dp * ROWS
    positions = lax.broadcasted_iota(jnp.int32, (ROWS, TOK), 0) + first_row
    for g in range(N_DP):
        logits = total[:, g * TOK : (g + 1) * TOK]
        digits = cot_ref[g, ROWS : ROWS + 3].astype(F32)
        target = (digits[0:1] * 16384.0 + digits[1:2] * 128.0 + digits[2:3]).astype(jnp.int32)
        top = jnp.max(logits, axis=0, keepdims=True)
        sums = jnp.sum(jnp.exp(logits - top), axis=0, keepdims=True)
        picked = jnp.sum(jnp.where(positions == target, logits, 0.0), axis=0, keepdims=True)
        rest = jnp.concatenate([top, sums, picked], axis=0)
        rows = []
        for _ in range(3):
            rows.append(rest.astype(BF16).astype(F32))
            rest = rest - rows[-1]
        rows.append(jnp.zeros((EXTRA - 9, TOK), F32))
        out_ref[g, :ROWS] = logits.astype(BF16)
        out_ref[g, ROWS:] = jnp.concatenate(rows, axis=0).astype(BF16)


def update_and_logits(place, now_next, mine, other, cot, state):
    whole = (N_DP, ROWS + EXTRA, TOK)
    placed = [pinned(v) if late else in_hbm(v) for values in (mine, other) for v, late in zip(values, LATE)]
    width = state[0].shape[1]
    return pl.pallas_call(
        update_kernel,
        out_shape=jax.ShapeDtypeStruct(whole, BF16),
        in_specs=[SMEM, HBM, HBM] + [ANY] * (len(mine) + len(other)) + [VMEM] + [HBM] * 3,
        out_specs=VMEM,
        scratch_shapes=[
            pltpu.VMEM((ROWS, N_DP * TOK), BF16),
            pltpu.VMEM((2, N_DP * TOK, width), BF16),
            *[pltpu.VMEM(v.shape, v.dtype) for v in state],
            pltpu.VMEM((ROWS, N_DP * TOK), F32),
            pltpu.SemaphoreType.DMA((width // BLOCK,)),
        ],
        compiler_params=pltpu.CompilerParams(vmem_limit_bytes=32 * MIB),
        cost_estimate=pl.CostEstimate(flops=9_400_000_000, bytes_accessed=24_000_000, transcendentals=2_300_000),
        name="update_and_logits",
    )(place, *[in_hbm(v) for v in now_next], *placed, cot, *[in_hbm(v) for v in state])


def turn_kernel(part_ref, out_ref):
    rows = jnp.concatenate([part_ref[g, :ROWS] for g in range(N_DP)], axis=0)
    out_ref[...] = rows.T


def turn(parts):
    return pl.pallas_call(
        turn_kernel,
        out_shape=jax.ShapeDtypeStruct((TOK, N_DP * ROWS), BF16),
        in_specs=[VMEM],
        out_specs=VMEM,
        compiler_params=pltpu.CompilerParams(vmem_limit_bytes=4 * MIB),
        cost_estimate=pl.CostEstimate(flops=0, bytes_accessed=1_400_000, transcendentals=0),
        name="turn",
    )(parts)


def merged(value):
    top, sums, picked = value[:, 0], value[:, 1], value[:, 2]
    row_top = jnp.max(top, axis=0, keepdims=True)
    row_total = jnp.sum(sums * jnp.exp(top - row_top), axis=0, keepdims=True)
    return row_top, row_total, jnp.sum(picked, axis=0, keepdims=True)


def merge_kernel(part_ref, out_ref, extra, sem):
    load = pltpu.make_async_copy(part_ref.at[:, pl.ds(ROWS, EXTRA), :], extra, sem)
    load.start()
    load.wait()
    rows = extra[...].astype(F32)
    value = rows[:, 0:3] + rows[:, 3:6] + rows[:, 6:9]
    out_ref[...] = jnp.broadcast_to(jnp.concatenate(merged(value), axis=0)[None], out_ref.shape)


def merge(parts):
    return pl.pallas_call(
        merge_kernel,
        out_shape=jax.ShapeDtypeStruct((N_VOCAB, 3, TOK), F32),
        in_specs=[ANY],
        out_specs=VMEM,
        scratch_shapes=[pltpu.VMEM((N_DP, EXTRA, TOK), BF16), pltpu.SemaphoreType.DMA(())],
        compiler_params=pltpu.CompilerParams(vmem_limit_bytes=4 * MIB),
        name="merge",
    )(parts)


def loss_kernel(stat_ref, out_ref):
    row_top, row_total, picked = merged(stat_ref[...])
    out_ref[...] = jnp.log(row_total) + row_top - picked


def loss(stat):
    out = pl.pallas_call(
        loss_kernel,
        out_shape=jax.ShapeDtypeStruct((1, TOK), F32),
        in_specs=[VMEM],
        out_specs=VMEM,
        compiler_params=pltpu.CompilerParams(vmem_limit_bytes=4 * MIB),
        name="loss",
    )(stat)
    return out.reshape(TOK)


def shards(hidden_now, hidden_next, cotangent, master, moment, second, targets):
    dp, vocab = lax.axis_index("dp"), lax.axis_index("vocab")
    place = jnp.stack([vocab % NC, (vocab // (NZH * NC)) % 2, dp, vocab]).astype(jnp.int32)
    to_x, to_z = arrange(place, hidden_now, hidden_next)
    mine, other, cot = gather(to_x, to_z, prepare(cotangent, targets))
    parts = update_and_logits(place, (hidden_now, hidden_next), mine, other, cot, (master, moment, second))
    parts = lax.all_to_all(parts, "dp", 0, 0)
    stat = lax.all_to_all(merge(parts), "vocab", 0, 0)
    return turn(parts), loss(stat)


def solution(mesh):
    in_specs = (
        P("dp", None),
        P("dp", None),
        P("dp", "vocab"),
        P(("vocab", "dp"), None),
        P(("vocab", "dp"), None),
        P(("vocab", "dp"), None),
        P("dp"),
    )
    out_specs = (P("dp", "vocab"), P("dp"))
    return jax.shard_map(shards, mesh=mesh, in_specs=in_specs, out_specs=out_specs, check_vma=False)
```

```python
import functools

import jax
import jax.numpy as jnp
from jax import lax
from jax.experimental import pallas as pl
from jax.experimental.pallas import tpu as pltpu
from jax.sharding import PartitionSpec as P

learn_rate = 0.02
beta_one = 0.9
beta_two = 0.95
epsilon = 1e-08
decay_rate = 0.1

NX, NZL, NY, NZH, NC = 4, 2, 4, 4, 2
NZ = NZL * NZH
N_DP, N_VOCAB = NX * NZL, NY * NZH * NC
TOK = 128
HALF = TOK // 2
CHUNK = 16
ROWS = 320
BLOCK = 512
MIB = 2**20
BF16 = jnp.bfloat16
F32 = jnp.float32


def device_number(x, y, z, core):
    return ((z % NZL) * NX + x) * N_VOCAB + (y * NZH + z // NZL) * NC + core


def receive(value, axes):
    pairs = []
    for x in range(NX):
        for y in range(NY):
            for z in range(NZ):
                for core in range(NC):
                    step = 1 - 2 * core
                    if axes == "core":
                        source = device_number(x, y, z, 1 - core)
                    else:
                        dx, dy, dz = (step if axis in axes else 0 for axis in "xyz")
                        source = device_number((x + dx) % NX, (y + dy) % NY, (z - dz) % NZ, core)
                    pairs.append((source, device_number(x, y, z, core)))
    return lax.ppermute(value, ("dp", "vocab"), pairs)


FIRST, SECOND = 0, 1
OWN, OTHER = 0, 1
HERE, SIDE, ACROSS = 0, 1, 2
CONTENTS = (
    ((0, SIDE, FIRST, OWN), (0, SIDE, FIRST, OTHER)),
    ((1, HERE, FIRST, OWN), (1, HERE, SECOND, OWN)),
    ((0, SIDE, SECOND, OWN), (0, SIDE, SECOND, OTHER)),
    ((1, SIDE, FIRST, OWN), (1, SIDE, FIRST, OTHER)),
    ((0, ACROSS, FIRST, OWN), (1, SIDE, SECOND, OWN)),
    ((0, ACROSS, SECOND, OWN), (1, SIDE, SECOND, OTHER)),
    ((1, ACROSS, SECOND, OWN), (1, ACROSS, FIRST, OWN)),
)


def pinned(value):
    return pltpu.with_memory_space_constraint(value, pltpu.VMEM)


def in_hbm(value):
    return pltpu.with_memory_space_constraint(value, pltpu.HBM)


VMEM = pl.BlockSpec(memory_space=pltpu.VMEM)
SMEM = pl.BlockSpec(memory_space=pltpu.SMEM)
HBM = pl.BlockSpec(memory_space=pltpu.HBM)
ANY = pl.BlockSpec(memory_space=pl.ANY)


def copy_rows(copies, sem):
    started = []
    for source, at, target, to in copies:
        for row in range(0, HALF, CHUNK):
            started.append(
                pltpu.make_async_copy(
                    source.at[pl.ds(pl.multiple_of(at + row, CHUNK), CHUNK)],
                    target.at[pl.ds(to + row, CHUNK)],
                    sem.at[len(started)],
                )
            )
    for each in started:
        each.start()
    for each in started:
        each.wait()


LATE = (False, False, False, False, False, True, True)


def arrange_kernel(place, now_ref, next_ref, x_ref, z_ref, sem):
    core, odd = place[0], place[1]
    own, other = core * HALF, (1 - core) * HALF

    def copy(first_ref, second_ref):
        copy_rows(
            ((first_ref, own, x_ref, 0), (second_ref, own, z_ref, HALF), (first_ref, other, x_ref, HALF)), sem
        )
        z_ref[:HALF] = x_ref[:HALF]

    @pl.when(odd == 0)
    def _():
        copy(now_ref, next_ref)

    @pl.when(odd == 1)
    def _():
        copy(next_ref, now_ref)


def arrange(place, hidden_now, hidden_next):
    return pl.pallas_call(
        arrange_kernel,
        out_shape=(pltpu.VMEM(hidden_now.shape, BF16),) * 2,
        in_specs=[SMEM, HBM, HBM],
        out_specs=(VMEM,) * 2,
        scratch_shapes=[pltpu.SemaphoreType.DMA((4 * HALF // CHUNK,))],
        compiler_params=pltpu.CompilerParams(vmem_limit_bytes=4 * MIB),
        name="arrange",
    )(place, in_hbm(hidden_now), in_hbm(hidden_next))


EXTRA = 16


def prepare_kernel(cot_ref, target_ref, out_ref):
    turned = cot_ref[...].T
    target = target_ref[...]
    digits = [target // 16384, (target // 128) % 128, target % 128]
    rows = jnp.concatenate(digits + [jnp.zeros((EXTRA - 3, TOK), jnp.int32)], axis=0)
    rows = rows.astype(F32).astype(BF16)
    for g in range(N_DP):
        out_ref[g, :ROWS] = turned[g * ROWS : (g + 1) * ROWS]
        out_ref[g, ROWS:] = rows


def prepare(cotangent, targets):
    return pl.pallas_call(
        prepare_kernel,
        out_shape=jax.ShapeDtypeStruct((N_DP, ROWS + EXTRA, TOK), BF16),
        in_specs=[VMEM, VMEM],
        out_specs=VMEM,
        compiler_params=pltpu.CompilerParams(vmem_limit_bytes=2 * MIB),
        name="prepare",
    )(cotangent, targets.reshape(1, TOK))


def second_round_kernel(x1_ref, z1_ref, x_ref, sem):
    load = pltpu.make_async_copy(z1_ref.at[pl.ds(HALF, HALF)], x_ref.at[pl.ds(HALF, HALF)], sem)
    load.start()
    x_ref[:HALF] = x1_ref[:HALF]
    load.wait()


def third_round_kernel(x2_ref, z2_ref, x_ref, y_ref):
    x_ref[:HALF] = x2_ref[HALF:]
    x_ref[HALF:] = z2_ref[:HALF]
    y_ref[:HALF] = x2_ref[:HALF]
    y_ref[HALF:] = z2_ref[HALF:]


def rearranged(kernel, values, outputs, in_specs, scratch=()):
    return pl.pallas_call(
        kernel,
        out_shape=(pltpu.VMEM(values[0].shape, BF16),) * outputs,
        in_specs=in_specs,
        out_specs=(VMEM,) * outputs,
        scratch_shapes=scratch,
        compiler_params=pltpu.CompilerParams(vmem_limit_bytes=4 * MIB),
        name="rearranged",
    )(*values)


def gather(to_x, to_z, cot):
    swap = lambda v: receive(v, "core")
    x1, z1 = receive(to_x, "x"), receive(to_z, "z")
    cot, _ = lax.optimization_barrier((cot, x1))
    cot = lax.all_to_all(cot, "dp", 0, 0)
    y2, z2 = receive(x1, "y"), receive(x1, "z")
    (to_x,) = rearranged(
        second_round_kernel, (pinned(x1), z1), 1, [VMEM, ANY], [pltpu.SemaphoreType.DMA(())]
    )
    x2 = receive(to_x, "x")
    y2, z2, x2, cot = lax.optimization_barrier((y2, z2, x2, cot))
    to_x, to_y = rearranged(third_round_kernel, (pinned(x2), pinned(z2)), 2, [VMEM, VMEM])
    y3, x3 = receive(to_y, "y"), receive(to_x, "x")
    mine = [x1, z1, y2, z2, x2, y3, x3]
    return mine, [swap(v) for v in mine], cot


def update_kernel(place, now_ref, next_ref, *refs):
    n = 2 * len(CONTENTS)
    pieces, (cot_ref, *state), (out_ref, cot_t, hidden, *kept, total, sems) = refs[:n], refs[n : n + 4], refs[n + 4 :]
    steps = kept[0].shape[1] // BLOCK
    core, odd, dp, vocab = place[0], place[1], place[2], place[3]
    zl, x = dp // NX, lax.rem(dp, NX)
    rank_of = lambda dz, dx: (lax.rem(zl + dz, NZL)) * NX + lax.rem(x + dx, NX)

    copies = [(now_ref, 0, 0, dp * TOK, TOK), (next_ref, 0, 1, dp * TOK, TOK)]
    for group, half in ((0, core), (1, 1 - core)):
        x_at = (0, 1 + 2 * half, 2)
        for number, contents in enumerate(CONTENTS):
            for part, (dz, dx, array, which) in enumerate(contents):
                token = rank_of(dz, x_at[dx]) * TOK + (1 - half if which == OTHER else half) * HALF
                ref = pieces[group * len(CONTENTS) + number]
                copies.append((ref, part * HALF, 1 - odd if array == SECOND else odd, token, HALF))
    columns = lambda step: pl.ds(step * BLOCK, BLOCK)

    for step in range(steps):
        for ref, row, array, token, rows in copies:
            pltpu.make_async_copy(
                ref.at[pl.ds(row, rows), columns(step)],
                hidden.at[array, pl.ds(pl.multiple_of(token, HALF), rows), columns(step)],
                sems.at[step],
            ).start()
        for source, target in zip(state, kept):
            pltpu.make_async_copy(source.at[:, columns(step)], target.at[:, columns(step)], sems.at[step]).start()

    for g in range(N_DP):
        cot_t[:, g * TOK : (g + 1) * TOK] = cot_ref[g, :ROWS]
    def gradient_of(step):
        for ref in (hidden, *kept):
            now = ref.at[..., columns(step)]
            pltpu.make_async_copy(now, now, sems.at[step]).wait()
        return jnp.dot(cot_t[...], hidden[0, :, columns(step)], preferred_element_type=F32)

    following = gradient_of(0)
    for step in range(steps):
        gradient = following
        if step + 1 < steps:
            following = gradient_of(step + 1)
        master, moment, second = (target[:, columns(step)].astype(F32) for target in kept)
        moment_new = beta_one * moment + (1.0 - beta_one) * gradient
        second_new = beta_two * second + (1.0 - beta_two) * gradient * gradient
        root = second_new * lax.rsqrt(second_new)
        scale = lax.rsqrt(second_new + epsilon * (2.0 * root + epsilon))
        rows_new = (1.0 - learn_rate * decay_rate) * master - learn_rate * (moment_new * scale)
        product = lax.dot_general(
            rows_new.astype(BF16), hidden[1, :, columns(step)], (((1,), (1,)), ((), ())), preferred_element_type=F32
        )
        if step == 0:
            total[...] = product
        else:
            total[...] += product

    first_row = vocab * (N_DP * ROWS) + dp * ROWS
    positions = lax.broadcasted_iota(jnp.int32, (ROWS, TOK), 0) + first_row
    for g in range(N_DP):
        logits = total[:, g * TOK : (g + 1) * TOK]
        digits = cot_ref[g, ROWS : ROWS + 3].astype(F32)
        target = (digits[0:1] * 16384.0 + digits[1:2] * 128.0 + digits[2:3]).astype(jnp.int32)
        top = jnp.max(logits, axis=0, keepdims=True)
        sums = jnp.sum(jnp.exp(logits - top), axis=0, keepdims=True)
        picked = jnp.sum(jnp.where(positions == target, logits, 0.0), axis=0, keepdims=True)
        rest = jnp.concatenate([top, sums, picked], axis=0)
        rows = []
        for _ in range(3):
            rows.append(rest.astype(BF16).astype(F32))
            rest = rest - rows[-1]
        rows.append(jnp.zeros((EXTRA - 9, TOK), F32))
        out_ref[g, :ROWS] = logits.astype(BF16)
        out_ref[g, ROWS:] = jnp.concatenate(rows, axis=0).astype(BF16)


def update_and_logits(place, now_next, mine, other, cot, state):
    whole = (N_DP, ROWS + EXTRA, TOK)
    placed = [pinned(v) if late else in_hbm(v) for values in (mine, other) for v, late in zip(values, LATE)]
    width = state[0].shape[1]
    return pl.pallas_call(
        update_kernel,
        out_shape=jax.ShapeDtypeStruct(whole, BF16),
        in_specs=[SMEM, HBM, HBM] + [ANY] * (len(mine) + len(other)) + [VMEM] + [HBM] * 3,
        out_specs=VMEM,
        scratch_shapes=[
            pltpu.VMEM((ROWS, N_DP * TOK), BF16),
            pltpu.VMEM((2, N_DP * TOK, width), BF16),
            *[pltpu.VMEM(v.shape, v.dtype) for v in state],
            pltpu.VMEM((ROWS, N_DP * TOK), F32),
            pltpu.SemaphoreType.DMA((width // BLOCK,)),
        ],
        compiler_params=pltpu.CompilerParams(vmem_limit_bytes=32 * MIB),
        cost_estimate=pl.CostEstimate(flops=9_400_000_000, bytes_accessed=24_000_000, transcendentals=2_300_000),
        name="update_and_logits",
    )(place, *[in_hbm(v) for v in now_next], *placed, cot, *[in_hbm(v) for v in state])


def turn_kernel(part_ref, out_ref):
    rows = jnp.concatenate([part_ref[g, :ROWS] for g in range(N_DP)], axis=0)
    out_ref[...] = rows.T


def turn(parts):
    return pl.pallas_call(
        turn_kernel,
        out_shape=jax.ShapeDtypeStruct((TOK, N_DP * ROWS), BF16),
        in_specs=[VMEM],
        out_specs=VMEM,
        compiler_params=pltpu.CompilerParams(vmem_limit_bytes=4 * MIB),
        cost_estimate=pl.CostEstimate(flops=0, bytes_accessed=1_400_000, transcendentals=0),
        name="turn",
    )(parts)


def merged(value):
    top, sums, picked = value[:, 0], value[:, 1], value[:, 2]
    row_top = jnp.max(top, axis=0, keepdims=True)
    row_total = jnp.sum(sums * jnp.exp(top - row_top), axis=0, keepdims=True)
    return row_top, row_total, jnp.sum(picked, axis=0, keepdims=True)


def merge_kernel(part_ref, out_ref, extra, sem):
    load = pltpu.make_async_copy(part_ref.at[:, pl.ds(ROWS, EXTRA), :], extra, sem)
    load.start()
    load.wait()
    rows = extra[...].astype(F32)
    value = rows[:, 0:3] + rows[:, 3:6] + rows[:, 6:9]
    out_ref[...] = jnp.broadcast_to(jnp.concatenate(merged(value), axis=0)[None], out_ref.shape)


def merge(parts):
    return pl.pallas_call(
        merge_kernel,
        out_shape=jax.ShapeDtypeStruct((N_VOCAB, 3, TOK), F32),
        in_specs=[ANY],
        out_specs=VMEM,
        scratch_shapes=[pltpu.VMEM((N_DP, EXTRA, TOK), BF16), pltpu.SemaphoreType.DMA(())],
        compiler_params=pltpu.CompilerParams(vmem_limit_bytes=4 * MIB),
        name="merge",
    )(parts)


def loss_kernel(stat_ref, out_ref):
    row_top, row_total, picked = merged(stat_ref[...])
    out_ref[...] = jnp.log(row_total) + row_top - picked


def loss(stat):
    out = pl.pallas_call(
        loss_kernel,
        out_shape=jax.ShapeDtypeStruct((1, TOK), F32),
        in_specs=[VMEM],
        out_specs=VMEM,
        compiler_params=pltpu.CompilerParams(vmem_limit_bytes=4 * MIB),
        name="loss",
    )(stat)
    return out.reshape(TOK)


def shards(hidden_now, hidden_next, cotangent, master, moment, second, targets):
    dp, vocab = lax.axis_index("dp"), lax.axis_index("vocab")
    place = jnp.stack([vocab % NC, (vocab // (NZH * NC)) % 2, dp, vocab]).astype(jnp.int32)
    to_x, to_z = arrange(place, hidden_now, hidden_next)
    mine, other, cot = gather(to_x, to_z, prepare(cotangent, targets))
    parts = update_and_logits(place, (hidden_now, hidden_next), mine, other, cot, (master, moment, second))
    parts = lax.all_to_all(parts, "dp", 0, 0)
    stat = lax.all_to_all(merge(parts), "vocab", 0, 0)
    return turn(parts), loss(stat)


def solution(mesh):
    in_specs = (
        P("dp", None),
        P("dp", None),
        P("dp", "vocab"),
        P(("vocab", "dp"), None),
        P(("vocab", "dp"), None),
        P(("vocab", "dp"), None),
        P("dp"),
    )
    out_specs = (P("dp", "vocab"), P("dp"))
    return jax.shard_map(shards, mesh=mesh, in_specs=in_specs, out_specs=out_specs, check_vma=False)
```
